128 devices in a mesh: rows: 8 (over z, core), seq: 16 (over y, x).
Axes of the slice: x: 4, y: 4, z: 4, core: 2. Of those that a mesh axis runs over, the one named last changes fastest.
Arguments:
- acts: bfloat16 [16, 2048, 512], P('rows', 'seq'), may hold values from -6 to 6
- segment_ids: int32 [16, 2048], P('rows', 'seq'), may hold values from 0 to 3, as said below
- cotangent: bfloat16 [16, 2048, 512], P('rows', 'seq'), may hold values from -6 to 6
- norm_one: float32 [2, 512], replicated, may hold values from 0.5 to 1.5
- w_in: bfloat16 [2, 512, 1024], replicated, may hold values from -0.25 to 0.25
- taps: float32 [2, 8, 16, 512], P(None, 'rows'), may hold values from -9 to 9
- skip_gain: float32 [2, 512], replicated, may hold values from -1 to 1
- w_out: bfloat16 [2, 512, 512], replicated, may hold values from -0.25 to 0.25
- norm_two: float32 [2, 512], replicated, may hold values from 0.5 to 1.5
- w_up: bfloat16 [2, 512, 2048], replicated, may hold values from -0.25 to 0.25
- w_down: bfloat16 [2, 2048, 512], replicated, may hold values from -0.125 to 0.125
Outputs:
- act_out: float32 [16, 2048, 512], P('rows', 'seq')
- grad_input: float32 [16, 2048, 512], P('rows', 'seq')
- grad_norm_one: float32 [2, 512], P(None, ('rows', 'seq'))
- grad_w_in: float32 [2, 512, 1024], P(None, ('rows', 'seq'))
- grad_taps: float32 [2, 8, 16, 512], P(None, 'rows')
- grad_skip: float32 [2, 512], P(None, ('rows', 'seq'))
- grad_w_out: float32 [2, 512, 512], P(None, ('rows', 'seq'))
- grad_norm_two: float32 [2, 512], P(None, ('rows', 'seq'))
- grad_w_up: float32 [2, 512, 2048], P(None, ('rows', 'seq'))
- grad_w_down: float32 [2, 2048, 512], P(None, ('rows', 'seq'))
The draws below stay inside these ranges and needn't reach their ends.
Inputs may be any that keep to these rules, and one draw needn't show every extreme that they name: `segment_ids`: non-decreasing along each row.
All inputs are finite; a program needn't handle non-finite values.
Results may differ from the reference program's by a relative error of at most 0.02.
Values sent between devices are 32-bit elements; how exact they have to be, the bound alone decides.
No kernel may reach another device: no remote copies, remote signals or barrier semaphores. Data moves between devices by JAX's collectives and lax.ppermute only.
A program may use at most 256 MiB of HBM per device.

```python
import jax
import jax.numpy as jnp
from jax import lax

D = 512
FF = 2048
NSCALE = 8
DOCS = 4
LAYERS = 2
L = 2048
KDIM = 16
ROWS = 16
N_ROWS = 8
N_SEQ = 16


def draw_segment_ids(key, part):
    key = jax.random.fold_in(key, 11)
    key_long, key_early, key_late, key_free, key_pick = jax.random.split(key, 5)
    span = L // N_SEQ
    group = ROWS // N_ROWS
    longest = jax.random.randint(key_long, (ROWS, 1), 0, DOCS)
    early = jax.random.randint(key_early, (ROWS, DOCS - 1), 1, span)
    late = jax.random.randint(key_late, (ROWS, DOCS - 1), L - span + 1, L)
    boundary = jnp.arange(DOCS - 1, dtype=jnp.int32)[None, :]
    cuts_edge = jnp.sort(jnp.where(boundary < longest, early, late), axis=1)
    cuts_free = jnp.sort(jax.random.randint(key_free, (ROWS, DOCS - 1), 1, L), axis=1)
    chosen = jnp.repeat(jax.random.randint(key_pick, (N_ROWS,), 0, group), group)
    slot = jnp.arange(ROWS, dtype=jnp.int32) % group
    cuts = jnp.where((slot == chosen)[:, None], cuts_edge, cuts_free)
    positions = jnp.arange(L, dtype=jnp.int32)[None, :, None]
    return jnp.sum((positions >= cuts[:, None, :]).astype(jnp.int32), axis=2).astype(jnp.int32)


def draw_taps(key, part):
    key = jax.random.fold_in(key, 5)
    base = jax.random.truncated_normal(key, -3.0, 3.0, (LAYERS, NSCALE, KDIM, D), jnp.float32)
    return base


def levels(rng, dims, cuts, least, high):
    factor_of = 1.0
    for position, parts in cuts:
        steps = jax.random.uniform(jax.random.fold_in(jax.random.fold_in(rng, 6), position), (parts,), jnp.float32, least / len(cuts), high / len(cuts))
        factor_of = factor_of * jnp.repeat(jnp.exp(steps), dims[position] // parts).reshape((-1,) + (1,) * (len(dims) - 1 - position))
    return factor_of


def scatter_about(key, extent, width, reach, cuts=(), kind=jnp.bfloat16):
    entries = width * jax.random.normal(key, extent, jnp.float32)
    if cuts:
        entries = entries * levels(key, extent, cuts, -0.22, 0.18)
    return jnp.clip(entries, -reach, reach).astype(kind)


def setup_inputs(seed: int = 0) -> dict:
    key_list = jax.random.split(jax.random.key(seed), 12)
    acts = scatter_about(key_list[0], (ROWS, L, D), 1.0, 6.0, ((0, 8), (1, 16)))
    segment_ids = draw_segment_ids(jax.random.fold_in(key_list[11], 71), 0)
    cotangent = scatter_about(key_list[2], (ROWS, L, D), 1.0, 6.0, ((0, 8), (1, 16)))
    norm_one = jnp.clip(1.0 + 0.1 * jax.random.normal(key_list[3], (LAYERS, D), jnp.float32), 0.5, 1.5)
    w_in = scatter_about(key_list[4], (LAYERS, D, 2 * D), D ** -0.5, 0.25)
    taps = draw_taps(jax.random.fold_in(key_list[11], 71), 0)
    skip_gain = jnp.clip(jax.random.uniform(key_list[6], (LAYERS, D), jnp.float32, -1.0, 1.0), -1.0, 1.0)
    w_out = scatter_about(key_list[7], (LAYERS, D, D), D ** -0.5, 0.25)
    norm_two = jnp.clip(1.0 + 0.1 * jax.random.normal(key_list[8], (LAYERS, D), jnp.float32), 0.5, 1.5)
    w_up = scatter_about(key_list[9], (LAYERS, D, FF), D ** -0.5, 0.25)
    w_down = scatter_about(key_list[10], (LAYERS, FF, D), FF ** -0.5, 0.125)
    return {"acts": acts, "segment_ids": segment_ids, "cotangent": cotangent, "norm_one": norm_one, "w_in": w_in, "taps": taps, "skip_gain": skip_gain, "w_out": w_out, "norm_two": norm_two, "w_up": w_up, "w_down": w_down}


@jax.custom_vjp
def low(v):
    return lax.optimization_barrier(v.astype(jnp.bfloat16)).astype(jnp.float32)

@jax.custom_vjp
def low_back(v):
    return v

def low_keep(v):
    return (low(v), None)

def low_pass(kept, grad):
    return (grad,)

def back_keep(v):
    return (v, None)

def back_low(kept, grad):
    return (low(grad),)
low.defvjp(low_keep, low_pass)
low_back.defvjp(back_keep, back_low)
DECAY = 0.8
HIGHEST = lax.Precision.HIGHEST

def layer_norm(hidden_state, gain_row):
    centre = hidden_state - lax.optimization_barrier(jnp.mean(hidden_state, axis=-1, keepdims=True))
    spread = lax.optimization_barrier(jnp.mean(centre * centre, axis=-1, keepdims=True))
    return centre * lax.rsqrt(spread + 1e-05) * gain_row

def build_kernel(taps_layer):
    pieces = []
    for scale_index in range(NSCALE):
        repeat_count = max(1, 2 ** (scale_index - 1))
        pieces.append(jnp.repeat(taps_layer[scale_index], repeat_count, axis=0) * DECAY ** scale_index)
    raw_kernel = jnp.concatenate(pieces, axis=0)
    return raw_kernel * lax.rsqrt(lax.optimization_barrier(jnp.sum(raw_kernel * raw_kernel, axis=0)) + 1e-06)

def long_conv(values, kernel, segment_row):
    kernel_spectrum = jnp.fft.rfft(kernel, n=2 * L, axis=0)
    summed = jnp.zeros_like(values)
    for document in range(DOCS):
        inside = (segment_row == document).astype(values.dtype)[:, None]
        spectrum = jnp.fft.rfft(values * inside, n=2 * L, axis=0)
        summed = summed + inside * jnp.fft.irfft(spectrum * kernel_spectrum, n=2 * L, axis=0)[:L]
    return summed

def matmul_high(operand_one, operand_two):
    return jnp.dot(operand_one, operand_two, precision=HIGHEST, preferred_element_type=jnp.float32)

def row_forward(parameters, hidden_state, segment_row):
    gain_one, proj_in, tap_stack, skip_stack, proj_out, gain_two, proj_up, proj_down = parameters
    for layer_index in range(LAYERS):
        kernel = build_kernel(tap_stack[layer_index])
        normed_one = low(layer_norm(hidden_state, gain_one[layer_index]))
        mixed_proj = low_back(matmul_high(normed_one, proj_in[layer_index]))
        conv_values = low(mixed_proj[:, :D])
        gate_part = mixed_proj[:, D:]
        conv_out = long_conv(conv_values, kernel, segment_row) + skip_stack[layer_index] * conv_values
        gated_out = low(conv_out * jax.nn.gelu(gate_part))
        hidden_state = hidden_state + low_back(matmul_high(gated_out, proj_out[layer_index]))
        normed_two = low(layer_norm(hidden_state, gain_two[layer_index]))
        lifted = low_back(matmul_high(normed_two, proj_up[layer_index]))
        active = low(jax.nn.gelu(lifted))
        hidden_state = hidden_state + low_back(matmul_high(active, proj_down[layer_index]))
    return hidden_state

def reference(acts, segment_ids, cotangent, norm_one, w_in, taps, skip_gain, w_out, norm_two, w_up, w_down):
    parameters = tuple((item.astype(jnp.float32) for item in (norm_one, w_in, taps, skip_gain, w_out, norm_two, w_up, w_down)))

    def scan_step(totals, row_data):
        row_acts, row_segments, row_cotangent = row_data
        output, pullback = jax.vjp(lambda weights, inputs: row_forward(weights, inputs, row_segments), parameters, row_acts.astype(jnp.float32))
        gradients, grad_row = pullback(row_cotangent.astype(jnp.float32))
        totals = jax.tree.map(lambda first_sum, second_sum: first_sum + second_sum, totals, gradients)
        return (totals, (output, grad_row))
    zeros = jax.tree.map(jnp.zeros_like, parameters)
    totals, (outputs, grad_rows) = lax.scan(scan_step, zeros, (acts, segment_ids, cotangent))
    return (outputs, grad_rows, totals[0], totals[1], totals[2], totals[3], totals[4], totals[5], totals[6], totals[7])
```

```python
import math

import jax
import jax.numpy as jnp
import numpy as np
from jax import lax
from jax.experimental import pallas as pl
from jax.experimental.pallas import tpu as pltpu
from jax.sharding import PartitionSpec as P

D = 512
FF = 2048
NSCALE = 8
KDIM = 16
DOCS = 4
LAYERS = 2
BLOCK = 128
OWNED = 32
TOKENS = 256
DECAY = 0.8
F32 = jnp.float32
BF16 = jnp.bfloat16
ROOT = math.sqrt(2.0 / math.pi)
CUBE = 0.044715


def odd_angles(count):
    f = np.arange(128)
    n = np.arange(count)
    return np.pi * ((2 * f[None, :] + 1) * n[:, None] % 512) / 256.0


def build_tables(blocks):
    angles = odd_angles(256)
    cos, sin = np.cos(angles), np.sin(angles)
    into = np.concatenate([cos[:128], -sin[:128]], axis=1)
    back = np.concatenate([cos[128:], -sin[128:]], axis=1).T * (2.0 / 256.0)
    position = np.arange(blocks * BLOCK)
    scale = np.zeros_like(position)
    for level in range(1, NSCALE):
        scale += position >= KDIM * 2 ** (level - 1)
    repeat = 2 ** np.maximum(scale - 1, 0)
    start = np.where(scale == 0, 0, KDIM * repeat)
    tap = scale * KDIM + (position - start) // repeat
    chosen = np.zeros((NSCALE * KDIM, (blocks + 1) * BLOCK))
    chosen[tap, position + BLOCK] = 1.0
    window = np.concatenate([cos, -sin], axis=1)
    spectra = [chosen[:, BLOCK * d : BLOCK * (d + 2)] @ window for d in range(blocks)]
    return into, back, np.concatenate(spectra, axis=1)


TAP_DECAY = np.repeat(DECAY ** np.arange(NSCALE), KDIM)[:, None].astype(np.float32)
TAP_REPEAT = np.repeat([max(1, 2 ** (i - 1)) for i in range(NSCALE)], KDIM)[:, None].astype(np.float32)


def call(body, outs, args, scratch=(), smem=(), flops=0, limit=40):
    in_specs = [pl.BlockSpec(memory_space=pltpu.SMEM if i in smem else pltpu.VMEM) for i in range(len(args))]
    moved = sum(a.size * a.dtype.itemsize for a in args) + sum(math.prod(o[0]) * jnp.dtype(o[1]).itemsize for o in outs)
    return pl.pallas_call(
        body,
        out_shape=[jax.ShapeDtypeStruct(s, t) for s, t in outs],
        in_specs=in_specs,
        out_specs=[pl.BlockSpec(memory_space=pltpu.VMEM)] * len(outs),
        scratch_shapes=list(scratch),
        compiler_params=pltpu.CompilerParams(vmem_limit_bytes=limit * 2**20),
        cost_estimate=pl.CostEstimate(flops=flops, bytes_accessed=moved, transcendentals=0),
    )(*args)


def dot(a, b):
    return jnp.dot(a, b, preferred_element_type=F32)


def dot_nt(a, b):
    return lax.dot_general(a, b, (((1,), (1,)), ((), ())), preferred_element_type=F32)


def dot_tn(a, b):
    return lax.dot_general(a, b, (((0,), (0,)), ((), ())), preferred_element_type=F32)


def normalized(h):
    centre = h - jnp.mean(h, axis=-1, keepdims=True)
    scale = lax.rsqrt(jnp.mean(centre * centre, axis=-1, keepdims=True) + 1e-5)
    return centre * scale, scale


def norm_back(grad, h, gain):
    unit, scale = normalized(h)
    inner = grad * gain
    mean_one = jnp.mean(inner, axis=-1, keepdims=True)
    mean_two = jnp.mean(inner * unit, axis=-1, keepdims=True)
    return scale * (inner - mean_one - unit * mean_two)


def gelu_pair(x):
    t = jnp.tanh(ROOT * (x + CUBE * x * x * x))
    value = 0.5 * x * (1.0 + t)
    slope = 0.5 * (1.0 + t) + 0.5 * x * (1.0 - t * t) * (ROOT * (1.0 + 3.0 * CUBE * x * x))
    return value, slope


def spectra_kernel(taps, decay, repeat, table, values_out, norm_out, spectra_out):
    for l in range(LAYERS):
        raw = jnp.concatenate([taps[i, l] for i in range(NSCALE)], axis=0) * decay[...]
        norm = lax.rsqrt(jnp.sum(repeat[...] * raw * raw, axis=0, keepdims=True) + 1e-6)
        values = raw * norm
        values_out[l] = values
        norm_out[l] = norm
        spectra = jnp.dot(values.T, table[...], precision=lax.Precision.HIGHEST, preferred_element_type=F32)
        for d in range(spectra_out.shape[1]):
            spectra_out[l, d] = spectra[:, d * 256 : (d + 1) * 256]


def masked_stack(x, ids):
    return [jnp.where(ids == float(q), x, 0.0) for q in range(DOCS)]


def ids_of(seg, j, b):
    return seg[j, OWNED : OWNED + 1, b * 128 : (b + 1) * 128]


def transform(source, seg, table, out, blocks):
    for j in range(blocks):
        parts = []
        for b in range(2):
            parts += masked_stack(source[j, :OWNED, b * 128 : (b + 1) * 128], ids_of(seg, j, b))
        lhs = jnp.concatenate(parts, axis=0).astype(BF16)
        out[j] = dot(lhs, table[...]).reshape(out.shape[1:])


def halves(x):
    return x[..., :128], x[..., 128:]


def join(re, im):
    return jnp.concatenate([re, im], axis=-1)


def product(k, v):
    (kr, ki), (vr, vi) = halves(k), halves(v)
    return join(kr * vr - ki * vi, kr * vi + ki * vr)


def conj_product(k, v):
    (kr, ki), (vr, vi) = halves(k), halves(v)
    return join(kr * vr + ki * vi, kr * vi - ki * vr)


def block_sums(pairs, spectra, lag, signal, doc, times):
    totals = [None, None]
    for other in pairs:
        k = spectra[lag(other)]
        for b in range(2):
            term = times(k, signal[other, b, doc[b]])
            totals[b] = term if totals[b] is None else totals[b] + term
    return totals


def finish(mixed, seg, table, block, result):
    back = dot(mixed[...].reshape(256, 256).astype(BF16), table[...])
    for b in range(2):
        ids = ids_of(seg, block, b)
        total = None
        for q in range(DOCS):
            at = (b * DOCS + q) * OWNED
            piece = jnp.where(ids == float(q), back[at : at + OWNED], 0.0)
            total = piece if total is None else total + piece
        result(b, total)


def conv_kernel(forward, seg, ends, source, spectra, skip, into, back, out, signal, mixed):
    blocks = source.shape[0]
    times = product if forward else conj_product
    transform(source, seg, into, signal, blocks)
    for i in range(blocks):
        others = range(i) if forward else range(i + 1, blocks)
        doc = [ends[i, b] for b in range(2)]
        totals = block_sums(others, spectra, lambda o: abs(i - o), signal, doc, times)
        near = spectra[0]
        slot = i % 2
        for b in range(2):
            for q in range(DOCS):
                mixed[slot, b, q] = times(near, signal[i, b, q])
            if totals[b] is not None:
                mixed[slot, b, doc[b]] += totals[b]

        def result(b, total, i=i):
            at = pl.ds(b * 128, 128)
            out[i, :, at] = total + skip[...] * source[i, :OWNED, at]

        finish(mixed.at[slot], seg, back, i, result)


def conv_weight_kernel(seg, firsts, values, grads, into, into_grad, table, tap_values, out, signal, signal_grad, lines):
    blocks = values.shape[0]
    transform(values, seg, into, signal, blocks)
    transform(grads, seg, into_grad, signal_grad, blocks)
    for d in range(blocks):
        total = None
        for i in range(d, blocks):
            for b in range(2):
                for q in range(DOCS if d == 0 else 1):
                    at = q if d == 0 else firsts[i, b]
                    term = conj_product(signal[i - d, b, at], signal_grad[i, b, at])
                    total = term if total is None else total + term
        lines[:, d * 256 : (d + 1) * 256] = total
    sums = lax.dot_general(
        table[...], lines[...], (((1,), (1,)), ((), ())), precision=lax.Precision.HIGHEST, preferred_element_type=F32
    )
    aligned = jnp.sum(sums * tap_values[...], axis=0, keepdims=True)
    skip = jnp.zeros((OWNED, 256), F32)
    for j in range(blocks):
        skip += values[j, :OWNED] * grads[j]
    skip = lax.dot_general(
        jnp.ones((8, 256), F32), skip, (((1,), (1,)), ((), ())), precision=lax.Precision.HIGHEST, preferred_element_type=F32
    )
    row = lax.broadcasted_iota(jnp.int32, (8, OWNED), 0)
    extra = jnp.where(row == 0, skip, jnp.where(row == 1, aligned, 0.0))
    for i in range(NSCALE):
        out[i, :KDIM] = sums[i * KDIM : (i + 1) * KDIM]
        out[i, KDIM:] = extra


def project(h, gain, w_in, normed_out, gate_out, values_out):
    normed = (normalized(h)[0] * gain[...]).astype(BF16)
    normed_out[...] = normed
    values = dot(normed, w_in[:, :D]).astype(BF16).astype(F32)
    values_out[:, :OWNED] = values.T.reshape(values_out.shape[0], OWNED, TOKENS)
    gate_out[...] = dot(normed, w_in[:, D:])


def first_kernel(acts, seg, gain, w_in, normed_out, gate_out, values_out):
    project(acts[...].astype(F32), gain, w_in, normed_out, gate_out, values_out)
    ids = jnp.concatenate([seg[0:1], seg[1:2]], axis=1).astype(F32)
    values_out[:, OWNED:] = jnp.broadcast_to(ids[None], (values_out.shape[0], 8, TOKENS))


def mixer_and_ffn(conv, gate, h, w_out, gain, w_up, w_down, gated_out, middle_out, normed_out, active_out, slope_out, keep):
    conv_out = conv[...].reshape(D, 256).T
    value, slope = gelu_pair(gate[...])
    keep(value, conv_out * slope)
    gated = (conv_out * value).astype(BF16)
    gated_out[...] = gated
    middle = h[...].astype(F32) + dot(gated, w_out[...])
    middle_out[...] = middle
    normed = (normalized(middle)[0] * gain[...]).astype(BF16)
    normed_out[...] = normed
    total = middle
    for n in range(4):
        at = slice(n * 512, (n + 1) * 512)
        value, slope = gelu_pair(dot(normed, w_up[:, at]))
        active = value.astype(BF16)
        active_out[:, at] = active
        slope_out[:, at] = slope.astype(slope_out.dtype)
        total = total + dot(active, w_down[at, :])
    return total


def middle_kernel(conv, gate, h, w_out, gain_two, w_up, w_down, gain_one, w_in, gated_out, middle_out, normed_two_out, active_out,
                  slope_out, gate_value_out, gate_slope_out, state_out, normed_out, gate_out, values_out):
    def keep(value, slope):
        gate_value_out[...] = value
        gate_slope_out[...] = slope

    state = mixer_and_ffn(conv, gate, h, w_out, gain_two, w_up, w_down, gated_out, middle_out, normed_two_out, active_out, slope_out, keep)
    state_out[...] = state
    project(state, gain_one, w_in, normed_out, gate_out, values_out)


LOW, LIFTED, MID, GATE, GRADS = 0, D, D + FF, 2 * D + FF, 3 * D + FF


def rounded(x):
    return x.astype(BF16).astype(F32)


def ffn_back(grad_state, slope, middle, gain, w_up, w_down, w_out, gate_value, gate_slope, grads_out, grad_mid_out, grad_conv_out):
    grad_low = grad_state.astype(BF16)
    grads_out[:, LOW:LIFTED] = grad_low.astype(F32)
    grad_normed = None
    for n in range(4):
        at = slice(n * 512, (n + 1) * 512)
        grad_active = dot_nt(grad_low, w_down[at, :])
        lifted = (grad_active * slope[:, at].astype(F32)).astype(BF16)
        grads_out[:, LIFTED + n * 512 : LIFTED + (n + 1) * 512] = lifted.astype(F32)
        term = dot_nt(lifted, w_up[:, at])
        grad_normed = term if grad_normed is None else grad_normed + term
    grad_middle = grad_state + norm_back(grad_normed, middle[...], gain[...])
    grad_mid_out[...] = grad_middle
    low = grad_middle.astype(BF16)
    grads_out[:, MID:GATE] = low.astype(F32)
    grad_gated = dot_nt(low, w_out[...])
    grads_out[:, GATE:] = rounded(grad_gated * gate_slope[...])
    grad_conv_out[...] = (grad_gated * gate_value[...]).T.reshape(grad_conv_out.shape)


def top_kernel(conv, gate, h, w_out, gain_two, w_up, w_down, cotangent, act_out, gated_out, normed_two_out, active_out,
               grads_out, grad_mid_out, grad_conv_out, middle, slope, gate_value, gate_slope):
    def keep(value, slope_part):
        gate_value[...] = value
        gate_slope[...] = slope_part

    act_out[...] = mixer_and_ffn(conv, gate, h, w_out, gain_two, w_up, w_down, gated_out, middle, normed_two_out, active_out, slope, keep)
    ffn_back(cotangent[...].astype(F32), slope, middle, gain_two, w_up, w_down, w_out, gate_value, gate_slope,
             grads_out, grad_mid_out, grad_conv_out)


def mixer_back(grad_values, grads, grad_middle, h, gain, w_in, values_out):
    values = grad_values[...].reshape(D, TOKENS).T.astype(BF16)
    values_out[...] = values.astype(F32)
    grad_normed = dot_nt(values, w_in[:, :D]) + dot_nt(grads[:, GATE:].astype(BF16), w_in[:, D:])
    return grad_middle[...] + norm_back(grad_normed, h[...].astype(F32), gain[...])


def between_kernel(grad_values, grads, grad_middle, h, gain_one, w_in, slope, middle, gain_two, w_up, w_down, w_out, gate_value,
                   gate_slope, values_out, grads_out, grad_mid_out, grad_conv_out):
    state = mixer_back(grad_values, grads, grad_middle, h, gain_one, w_in, values_out)
    ffn_back(state, slope, middle, gain_two, w_up, w_down, w_out, gate_value, gate_slope, grads_out, grad_mid_out, grad_conv_out)


def last_kernel(grad_values, grads, grad_middle, h, gain_one, w_in, values_out, grad_out):
    grad_out[...] = mixer_back(grad_values, grads, grad_middle, h, gain_one, w_in, values_out)


def split_kernel(core, normed_one, gated, normed_two, active, own_out, send_out):
    first = core[0] == 0
    at = 0
    for x, step in ((normed_one, 64), (gated, 64), (normed_two, 64), (active, 256)):
        lines = x[...].astype(F32).T
        for z in range(4):
            even = lines[2 * z * step : (2 * z + 1) * step]
            odd = lines[(2 * z + 1) * step : (2 * z + 2) * step]
            own_out[at : at + step, :] = jnp.where(first, even, odd).astype(BF16)
            send_out[at : at + step, :] = jnp.where(first, odd, even)
            at += step


def store_wide(out, at, left, right):
    width = left.shape[1]
    left = left.reshape(32, 8, width)
    right = right.reshape(32, 8, width)
    low = lax.broadcasted_iota(jnp.int32, (32, 8, width), 1) < 4
    even = jnp.where(low, left, pltpu.roll(right, 4, 1))
    odd = jnp.where(low, pltpu.roll(left, 4, 1), right)
    both = jnp.stack([even, odd], axis=1).reshape(64, 8, width)
    for n in range(width // 128):
        out[:, at + n * 8 : at + (n + 1) * 8, :] = both[:, :, n * 128 : (n + 1) * 128]


def pair_product(own, other, rows, grads, other_grads, columns):
    return dot(own[rows, :], grads[:, columns].astype(BF16)) + dot(other[rows, :].astype(BF16), other_grads[:, columns].astype(BF16))


def wide_product(out, at, own, other, rows, grads, other_grads, left, right, width):
    left = pair_product(own, other, rows, grads, other_grads, slice(left, left + width))
    right = pair_product(own, other, rows, grads, other_grads, slice(right, right + width))
    store_wide(out, at, left, right)


ROWS_IN, ROWS_OUT, ROWS_UP, ROWS_DOWN = slice(0, 256), slice(256, 512), slice(512, 768), 768


def weight_kernel(*refs, late):
    if late:
        own, other, grads, other_grads, late_own, late_other, late_grads, late_other_grads, out_z, out_x, out_y = refs
    else:
        own, other, grads, other_grads, out_z, out_x, out_y = refs
    for n in range(4):
        rows = slice(ROWS_DOWN + n * 256, ROWS_DOWN + (n + 1) * 256)
        down = pair_product(own, other, rows, grads, other_grads, slice(LOW, LIFTED)).reshape(16, 16, D)
        for half in range(2):
            for lane in range(4):
                at = half * 32 + lane * 8
                out_z[n * 16 : (n + 1) * 16, at : at + 8, :] = down[:, half * 8 : half * 8 + 8, lane * 128 : (lane + 1) * 128]
    for n in range(4):
        target, at = (out_x, n * 16) if n < 3 else (out_y, 0)
        wide_product(target, at, own, other, ROWS_UP, grads, other_grads, LIFTED + n * 256, LIFTED + 1024 + n * 256, 256)
    wide_product(out_y, 16, own, other, ROWS_OUT, grads, other_grads, MID, MID + 256, 256)
    wide_product(out_y, 32, own, other, ROWS_IN, grads, other_grads, GATE, GATE + 256, 256)
    if late:
        wide_product(out_x, 48, late_own, late_other, ROWS_IN, late_grads, late_other_grads, 0, 256, 256)


def last_weight_kernel(own, other, grads, other_grads, out):
    wide_product(out, 0, own, other, ROWS_IN, grads, other_grads, 0, 256, 256)


def unpack_kernel(z_one, x_one, y_one, z_zero, x_zero, y_zero, tail, w_in, w_up, in_out, up_out, out_out, down_out, gain_one_out, gain_two_out):
    def wide(target, l, lines, at, column, gap):
        for n in range(2):
            for half in range(2):
                to = column + half * gap + n * 128
                target[l, :, to : to + 128] = lines[at + n * 8 + half * 4 : at + n * 8 + half * 4 + 4, :]

    for l, lines_z, lines_x, lines_y in ((0, z_zero, x_zero, y_zero), (1, z_one, x_one, y_one)):
        for half in range(2):
            for lane in range(4):
                at = half * 32 + lane * 8
                down_out[l, half * 8 : half * 8 + 8, lane * 128 : (lane + 1) * 128] = lines_z[at : at + 8, :]
        for n in range(4):
            source, at = (lines_x, n * 16) if n < 3 else (lines_y, 0)
            wide(up_out, l, source, at, n * 256, 1024)
        wide(out_out, l, lines_y, 16, 0, 256)
        wide(in_out, l, lines_y, 32, D, 256)
    wide(in_out, 0, tail, 0, 0, 256)
    wide(in_out, 1, x_zero, 48, 0, 256)
    for l in range(LAYERS):
        one = jnp.sum(in_out[l] * w_in[l].astype(F32), axis=1, keepdims=True)
        two = jnp.sum(up_out[l] * w_up[l].astype(F32), axis=1, keepdims=True)
        gain_one_out[l] = jnp.broadcast_to(one, (4, 128))
        gain_two_out[l] = jnp.broadcast_to(two, (4, 128))


def place(axis):
    rows, seq = lax.axis_index("rows"), lax.axis_index("seq")
    return {"z": rows // 2, "core": rows % 2, "y": seq // 4, "x": seq % 4}[axis]


def shift(x, axis, step):
    if axis == "core":
        return lax.ppermute(x, "rows", [(i, i ^ 1) for i in range(8)])
    if axis == "z":
        return lax.ppermute(x, "rows", [(i, (i + 2 * step) % 8) for i in range(8)])
    if axis == "y":
        return lax.ppermute(x, "seq", [(i, (i + 4 * step) % 16) for i in range(16)])
    return lax.ppermute(x, "seq", [(i, i // 4 * 4 + (i + step) % 4) for i in range(16)])


def taker(x, dim, axis):
    at = place(axis)
    return lambda step: lax.dynamic_index_in_dim(x, (at + step) % 4, dim, False)


def sum_direct(x, dim, axis):
    take = taker(x, dim, axis)
    return take(0) + shift(take(1), axis, 1) + shift(take(3), axis, 3) + shift(take(2), axis, 2)


def sum_ring(x, dim, axis):
    take = taker(x, dim, axis)
    middle = x.shape[-2] // 2
    first, second = lambda v: v[..., :middle, :], lambda v: v[..., middle:, :]
    far, right, left = take(2), take(1), take(3)
    from_left = shift(jnp.concatenate([first(far), second(right)], axis=-2), axis, 1)
    from_right = shift(jnp.concatenate([first(left), second(far)], axis=-2), axis, 3)
    on_left = shift(first(right) + first(from_left), axis, 1)
    on_right = shift(second(left) + second(from_right), axis, 3)
    here = take(0)
    return jnp.concatenate(
        [first(here) + first(from_right) + on_left, second(here) + second(from_left) + on_right], axis=-2
    )


def reduce_lines(lines, order):
    names = ["z", "y", "x"]
    total = lines.reshape(4, 4, 4, *lines.shape[1:])
    for n, axis in enumerate(order):
        total = (sum_ring if n == 0 else sum_direct)(total, names.index(axis), axis)
        names.remove(axis)
    return total


def gather_sum(x, axes):
    for axis in axes:
        if axis == "core":
            x = x + shift(x, axis, 1)
        else:
            x = x + shift(x, axis, 1) + shift(x, axis, 3) + shift(x, axis, 2)
    return x


def placed(x, at, length, dim):
    lengths = list(x.shape)
    lengths[dim] = length
    return lax.dynamic_update_slice_in_dim(jnp.zeros(lengths, x.dtype), x, at, dim)


def per_device(acts, segment_ids, cotangent, norm_one, w_in, taps, skip_gain, w_out, norm_two, w_up, w_down):
    seq = lax.axis_index("seq")
    rows = lax.axis_index("rows")
    blocks = lax.axis_size("seq")
    owner = (rows * blocks + seq) * 4
    core = place("core")[None]
    into_np, back_np, table_np = build_tables(blocks)
    into = jnp.asarray(into_np, BF16)
    back = jnp.asarray(back_np, BF16)
    into_grad = jnp.asarray(back_np.T, BF16)
    back_grad = jnp.asarray(into_np.T, BF16)
    table = jnp.asarray(table_np, F32)

    taps_here = lax.dynamic_slice_in_dim(taps[:, 0], seq * OWNED, OWNED, 2)
    taps_all = gather_sum(placed(taps_here[None], rows, NSCALE, 0), ("core", "z"))
    tap_values, norms, spectra = call(
        spectra_kernel,
        [((LAYERS, 128, OWNED), F32), ((LAYERS, 1, OWNED), F32), ((LAYERS, blocks, OWNED, 256), F32)],
        (taps_all, jnp.asarray(TAP_DECAY), jnp.asarray(TAP_REPEAT), table),
        flops=10**9,
    )
    skip_here = lax.dynamic_slice_in_dim(skip_gain, seq * OWNED, OWNED, 1)
    skip_here = jnp.broadcast_to(skip_here[:, :, None], (LAYERS, OWNED, 128))

    state = acts.reshape(TOKENS, D)
    exchange = (blocks, OWNED, TOKENS)
    wide = lambda n, t: ((TOKENS, n), t)
    gains = lambda g, l: g[l][None, :]

    def swap(x):
        return lax.all_to_all(x, "seq", 0, 0, tiled=True)

    normed_one, gate, values = call(
        first_kernel,
        [wide(D, BF16), wide(D, F32), ((blocks, OWNED + 8, TOKENS), F32)],
        (state, segment_ids, gains(norm_one, 0), w_in[0]),
        flops=2 * 10**9,
    )
    values_zero = seg = swap(values)
    ends = seg[:, OWNED, :].astype(jnp.int32).reshape(blocks, 2, BLOCK)
    firsts, lasts = ends[:, :, 0], ends[:, :, -1]

    def conv(l, forward, source):
        ends, first, second = (firsts, into, back) if forward else (lasts, into_grad, back_grad)
        (out,) = call(
            lambda *refs: conv_kernel(forward, *refs),
            [(exchange, F32)],
            (seg, ends, source, spectra[l], skip_here[l], first, second),
            scratch=[pltpu.VMEM((blocks, 2, DOCS, OWNED, 256), F32), pltpu.VMEM((2, 2, DOCS, OWNED, 256), F32)],
            smem=(1,),
            flops=4 * 10**9,
        )
        return out

    def split(*args):
        own, send = call(split_kernel, [((1792, TOKENS), BF16), ((1792, TOKENS), F32)], (core, *args), smem=(0,), flops=2 * 10**9)
        return own, shift(send, "core", 1)

    conv_zero = swap(conv(0, True, values_zero))
    (gated_zero, middle_zero, normed_two_zero, active_zero, slope_zero, gate_value_zero, gate_slope_zero, state_one, normed_one_one,
     gate_one, values_one) = call(
        middle_kernel,
        [wide(D, BF16), wide(D, F32), wide(D, BF16), wide(FF, BF16), wide(FF, BF16), wide(D, F32), wide(D, F32), wide(D, F32),
         wide(D, BF16), wide(D, F32), (exchange, F32)],
        (conv_zero, gate, state, w_out[0], gains(norm_two, 0), w_up[0], w_down[0], gains(norm_one, 1), w_in[1]),
        flops=4 * 10**9,
    )
    values_one = swap(values_one)
    left_zero = split(normed_one, gated_zero, normed_two_zero, active_zero)
    conv_one = swap(conv(1, True, values_one))
    back_outs = [wide(GRADS, F32), wide(D, F32), (exchange, F32)]
    act_out, gated_one, normed_two_one, active_one, grads_one, grad_mid, grad_conv = call(
        top_kernel,
        [wide(D, F32), wide(D, BF16), wide(D, BF16), wide(FF, BF16)] + back_outs,
        (conv_one, gate_one, state_one, w_out[1], gains(norm_two, 1), w_up[1], w_down[1], cotangent.reshape(TOKENS, D)),
        scratch=[pltpu.VMEM((TOKENS, D), F32), pltpu.VMEM((TOKENS, FF), BF16), pltpu.VMEM((TOKENS, D), F32), pltpu.VMEM((TOKENS, D), F32)],
        flops=5 * 10**9,
    )

    def pair_grads(grads):
        return grads, shift(grads, "core", 1)

    def weight_grads(left, grads, late=()):
        args = (*left, *grads, *late)
        shapes = [((64, n, 128), F32) for n in (64, 64 if late else 48, 48)]
        lines = call(lambda *refs: weight_kernel(*refs, late=bool(late)), shapes, args, flops=5 * 10**9)
        return [reduce_lines(x, order) for x, order in zip(lines, ("zyx", "xzy", "yxz"))]

    def conv_weights(l, source, grads):
        (out,) = call(
            conv_weight_kernel,
            [((NSCALE, KDIM + 8, OWNED), F32)],
            (seg, firsts, source, grads, into, into_grad, table, tap_values[l]),
            scratch=[pltpu.VMEM((blocks, 2, DOCS, OWNED, 256), F32)] * 2 + [pltpu.VMEM((OWNED, blocks * 256), F32)],
            smem=(1,),
            flops=4 * 10**9,
        )
        return out

    grad_conv = swap(grad_conv)
    left_one = split(normed_one_one, gated_one, normed_two_one, active_one)
    lines_one = weight_grads(left_one, pair_grads(grads_one))
    grad_values = swap(conv(1, False, grad_conv))
    tap_one = conv_weights(1, values_one, grad_conv)
    values_grad_one, grads_zero, grad_mid, grad_conv = call(
        between_kernel,
        [wide(D, F32)] + back_outs,
        (grad_values, grads_one, grad_mid, state_one, gains(norm_one, 1), w_in[1], slope_zero, middle_zero, gains(norm_two, 0), w_up[0],
         w_down[0], w_out[0], gate_value_zero, gate_slope_zero),
        flops=4 * 10**9,
    )
    grad_conv = swap(grad_conv)
    lines_zero = weight_grads(left_zero, pair_grads(grads_zero), (*left_one, *pair_grads(values_grad_one)))
    grad_values = swap(conv(0, False, grad_conv))
    tap_zero = conv_weights(0, values_zero, grad_conv)
    values_grad_zero, grad_input = call(
        last_kernel,
        [wide(D, F32), wide(D, F32)],
        (grad_values, grads_zero, grad_mid, state, gains(norm_one, 0), w_in[0]),
        flops=3 * 10**9,
    )
    (tail,) = call(last_weight_kernel, [((64, 16, 128), F32)], (*left_zero, *pair_grads(values_grad_zero)), flops=10**9)
    tail = reduce_lines(tail, "zyx")

    sums = jnp.stack([tap_zero, tap_one], axis=1)
    sums = sums.reshape(4, 2, *sums.shape[1:])
    mine = lax.dynamic_index_in_dim(sums, place("core"), 1, False)
    sums = mine + shift(lax.dynamic_index_in_dim(sums, 1 - place("core"), 1, False), "core", 1)
    sums = sum_direct(sums, 0, "z")
    decay = lax.dynamic_index_in_dim(jnp.asarray(TAP_DECAY[::KDIM, 0]), rows, 0, False)
    repeat = lax.dynamic_index_in_dim(jnp.asarray(TAP_REPEAT[::KDIM, 0]), rows, 0, False)
    own_values = taps_here * decay * norms
    tap_grad = decay * norms * (sums[:, :KDIM] - repeat * own_values * sums[:, KDIM + 1 : KDIM + 2])
    small = jnp.concatenate([tap_grad, sums[:, KDIM:]], axis=1)
    small = gather_sum(placed(small, seq * OWNED, D, 2), ("x", "y"))

    mine = lambda x, dim: lax.dynamic_slice_in_dim(x, owner, 4, dim)
    in_grad, up_grad, out_grad, down_grad, gain_one, gain_two = call(
        unpack_kernel,
        [((LAYERS, 4, 2 * D), F32), ((LAYERS, 4, FF), F32), ((LAYERS, 4, D), F32), ((LAYERS, 16, D), F32), ((LAYERS, 4, 128), F32),
         ((LAYERS, 4, 128), F32)],
        (*lines_one, *lines_zero, tail, mine(w_in, 1), mine(w_up, 1)),
    )
    return (
        act_out.reshape(acts.shape),
        grad_input.reshape(acts.shape),
        gain_one[:, :, 0] / mine(norm_one, 1),
        in_grad,
        small[:, None, :KDIM, :],
        mine(small[:, KDIM], 1),
        out_grad,
        gain_two[:, :, 0] / mine(norm_two, 1),
        up_grad,
        down_grad,
    )


def solution(mesh):
    wide = P("rows", "seq", None)
    in_specs = (wide, P("rows", "seq"), wide, P(), P(), P(None, "rows", None, None), P(), P(), P(), P(), P())
    split = P(None, ("rows", "seq"))
    split_wide = P(None, ("rows", "seq"), None)
    out_specs = (wide, wide, split, split_wide, P(None, "rows", None, None), split, split_wide, split, split_wide, split_wide)
    return jax.shard_map(per_device, mesh=mesh, in_specs=in_specs, out_specs=out_specs, check_vma=False)
```

```python
import math

import jax
import jax.numpy as jnp
import numpy as np
from jax import lax
from jax.experimental import pallas as pl
from jax.experimental.pallas import tpu as pltpu
from jax.sharding import PartitionSpec as P

D = 512
FF = 2048
NSCALE = 8
KDIM = 16
DOCS = 4
LAYERS = 2
BLOCK = 128
OWNED = 32
TOKENS = 256
DECAY = 0.8
F32 = jnp.float32
BF16 = jnp.bfloat16
ROOT = math.sqrt(2.0 / math.pi)
CUBE = 0.044715


def odd_angles(count):
    f = np.arange(128)
    n = np.arange(count)
    return np.pi * ((2 * f[None, :] + 1) * n[:, None] % 512) / 256.0


def build_tables(blocks):
    angles = odd_angles(256)
    cos, sin = np.cos(angles), np.sin(angles)
    into = np.concatenate([cos[:128], -sin[:128]], axis=1)
    back = np.concatenate([cos[128:], -sin[128:]], axis=1).T * (2.0 / 256.0)
    position = np.arange(blocks * BLOCK)
    scale = np.zeros_like(position)
    for level in range(1, NSCALE):
        scale += position >= KDIM * 2 ** (level - 1)
    repeat = 2 ** np.maximum(scale - 1, 0)
    start = np.where(scale == 0, 0, KDIM * repeat)
    tap = scale * KDIM + (position - start) // repeat
    chosen = np.zeros((NSCALE * KDIM, (blocks + 1) * BLOCK))
    chosen[tap, position + BLOCK] = 1.0
    window = np.concatenate([cos, -sin], axis=1)
    spectra = [chosen[:, BLOCK * d : BLOCK * (d + 2)] @ window for d in range(blocks)]
    return into, back, np.concatenate(spectra, axis=1)


TAP_DECAY = np.repeat(DECAY ** np.arange(NSCALE), KDIM)[:, None].astype(np.float32)
TAP_REPEAT = np.repeat([max(1, 2 ** (i - 1)) for i in range(NSCALE)], KDIM)[:, None].astype(np.float32)


class Fetched:
    def __init__(self, source, target, sem):
        self.copy = pltpu.make_async_copy(source, target, sem)
        self.copy.start()
        self.target = target
        self.shape = target.shape

    def __getitem__(self, at):
        if self.copy is not None:
            self.copy.wait()
            self.copy = None
        return self.target[at]


class Stored:
    def __init__(self, source, target, sem):
        self.source, self.target, self.sem = source, target, sem
        self.shape, self.dtype = source.shape, source.dtype
        self.copy = None

    def __setitem__(self, at, value):
        self.source[at] = value

    def __getitem__(self, at):
        return self.source[at]

    def send(self):
        if self.copy is None:
            self.copy = pltpu.make_async_copy(self.source, self.target, self.sem)
            self.copy.start()


def call(body, outs, args, scratch=(), flops=0, limit=56, raw=False):
    arrays = [a[0] if isinstance(a, tuple) else a for a in args]
    parts = [a[1] if isinstance(a, tuple) else () for a in args]
    seen = [jax.eval_shape(lambda x, p=p: x[p], a) if p is not None else None for a, p in zip(arrays, parts)]
    count = len(args)

    def kernel(*refs):
        sources, targets = refs[:count], refs[count : count + len(outs)]
        rest = list(refs[count + len(outs) :])
        loads, stores = rest.pop(), rest.pop()
        own_outs = [] if raw else [rest.pop() for _ in outs][::-1]
        own_ins = [None if v is None else rest.pop() for v in seen[::-1]][::-1]
        ins = [
            None if own is None else Fetched(source.at[part] if part != () else source, own, loads.at[i])
            for i, (source, own, part) in enumerate(zip(sources, own_ins, parts))
        ]
        results = [Stored(own, target, stores.at[i]) for i, (own, target) in enumerate(zip(own_outs, targets))]
        body(*[v for v in ins if v is not None], *(targets if raw else results), *rest)
        for v in ins:
            if v is not None and v.copy is not None:
                v.copy.wait()
        for r in results:
            r.send()
        for r in results:
            r.copy.wait()

    moved = sum(v.size * v.dtype.itemsize for v in seen if v is not None) + sum(math.prod(o[0]) * jnp.dtype(o[1]).itemsize for o in outs)
    return pl.pallas_call(
        kernel,
        out_shape=[jax.ShapeDtypeStruct(s, t) for s, t in outs],
        in_specs=[pl.BlockSpec(memory_space=pltpu.HBM)] * count,
        out_specs=[pl.BlockSpec(memory_space=pltpu.HBM)] * len(outs),
        scratch_shapes=[
            *scratch,
            *[pltpu.VMEM(v.shape, v.dtype) for v in seen if v is not None],
            *[pltpu.VMEM(s, t) for s, t in outs if not raw],
            pltpu.SemaphoreType.DMA((len(outs),)),
            pltpu.SemaphoreType.DMA((count,)),
        ],
        compiler_params=pltpu.CompilerParams(vmem_limit_bytes=limit * 2**20),
        cost_estimate=pl.CostEstimate(flops=flops, bytes_accessed=moved, transcendentals=0),
    )(*arrays)


def dot(a, b):
    return jnp.dot(a, b, preferred_element_type=F32)


def dot_nt(a, b):
    return lax.dot_general(a, b, (((1,), (1,)), ((), ())), preferred_element_type=F32)


def dot_tn(a, b):
    return lax.dot_general(a, b, (((0,), (0,)), ((), ())), preferred_element_type=F32)


def normalized(h):
    centre = h - jnp.mean(h, axis=-1, keepdims=True)
    scale = lax.rsqrt(jnp.mean(centre * centre, axis=-1, keepdims=True) + 1e-5)
    return centre * scale, scale


def norm_back(grad, h, gain):
    unit, scale = normalized(h)
    inner = grad * gain
    mean_one = jnp.mean(inner, axis=-1, keepdims=True)
    mean_two = jnp.mean(inner * unit, axis=-1, keepdims=True)
    return scale * (inner - mean_one - unit * mean_two)


def gelu_pair(x):
    t = jnp.tanh(ROOT * (x + CUBE * x * x * x))
    value = 0.5 * x * (1.0 + t)
    slope = 0.5 * (1.0 + t) + 0.5 * x * (1.0 - t * t) * (ROOT * (1.0 + 3.0 * CUBE * x * x))
    return value, slope


def spectra_kernel(taps, decay, repeat, table, *outs):
    for l in range(LAYERS):
        values_out, norm_out, spectra_out = outs[l], outs[LAYERS + l], outs[2 * LAYERS + l]
        raw = jnp.concatenate([taps[i, l * KDIM : (l + 1) * KDIM] for i in range(NSCALE)], axis=0) * decay[...]
        norm = lax.rsqrt(jnp.sum(repeat[...] * raw * raw, axis=0, keepdims=True) + 1e-6)
        values = raw * norm
        values_out[...] = values
        norm_out[...] = norm
        spectra = jnp.dot(values.T, table[...], precision=lax.Precision.HIGHEST, preferred_element_type=F32)
        for d in range(spectra_out.shape[0]):
            spectra_out[d] = spectra[:, d * 256 : (d + 1) * 256]


def masked_stack(x, ids):
    return [jnp.where(ids == float(q), x, 0.0) for q in range(DOCS)]


def ids_of(seg, j, b):
    return seg[j, OWNED : OWNED + 1, b * 128 : (b + 1) * 128]


def transform(source, seg, table, out, blocks):
    for j in range(blocks):
        parts = []
        for b in range(2):
            parts += masked_stack(source[j, :OWNED, b * 128 : (b + 1) * 128], ids_of(seg, j, b))
        lhs = jnp.concatenate(parts, axis=0).astype(BF16)
        out[j] = dot(lhs, table[...]).reshape(out.shape[1:])


def halves(x):
    return x[..., :128], x[..., 128:]


def join(re, im):
    return jnp.concatenate([re, im], axis=-1)


def product(k, v):
    (kr, ki), (vr, vi) = halves(k), halves(v)
    return join(kr * vr - ki * vi, kr * vi + ki * vr)


def conj_product(k, v):
    (kr, ki), (vr, vi) = halves(k), halves(v)
    return join(kr * vr + ki * vi, kr * vi - ki * vr)


def block_sums(pairs, spectra, lag, signal, doc, times):
    totals = [None, None]
    for other in pairs:
        k = spectra[lag(other)]
        for b in range(2):
            term = times(k, signal[other, b, doc[b]])
            totals[b] = term if totals[b] is None else totals[b] + term
    return totals


def finish(mixed, seg, table, block, result):
    back = dot(mixed[...].reshape(256, 256).astype(BF16), table[...])
    for b in range(2):
        ids = ids_of(seg, block, b)
        total = None
        for q in range(DOCS):
            at = (b * DOCS + q) * OWNED
            piece = jnp.where(ids == float(q), back[at : at + OWNED], 0.0)
            total = piece if total is None else total + piece
        result(b, total)


def edge_documents(seg, blocks, lane):
    def read(j, b):
        at = b * BLOCK + lane
        return jnp.sum(seg[j, OWNED : OWNED + 1, at : at + 1]).astype(jnp.int32)

    return [[read(j, b) for b in range(2)] for j in range(blocks)]


def conv_kernel(forward, seg, source, into, spectra, skip, back, out, signal, mixed):
    blocks = source.shape[0]
    ends = edge_documents(seg, blocks, 0 if forward else BLOCK - 1)
    times = product if forward else conj_product
    transform(source, seg, into, signal, blocks)
    for i in range(blocks):
        others = range(i) if forward else range(i + 1, blocks)
        doc = ends[i]
        totals = block_sums(others, spectra, lambda o: abs(i - o), signal, doc, times)
        near = spectra[0]
        slot = i % 2
        for b in range(2):
            for q in range(DOCS):
                mixed[slot, b, q] = times(near, signal[i, b, q])
            if totals[b] is not None:
                mixed[slot, b, doc[b]] += totals[b]

        def result(b, total, i=i):
            at = pl.ds(b * 128, 128)
            out[i, :, at] = total + skip[...] * source[i, :OWNED, at]

        finish(mixed.at[slot], seg, back, i, result)


def conv_weight_kernel(seg, values, grads, into, into_grad, table, tap_values, out, signal, signal_grad, lines):
    blocks = values.shape[0]
    firsts = edge_documents(seg, blocks, 0)
    transform(values, seg, into, signal, blocks)
    transform(grads, seg, into_grad, signal_grad, blocks)
    for d in range(blocks):
        total = None
        for i in range(d, blocks):
            for b in range(2):
                for q in range(DOCS if d == 0 else 1):
                    at = q if d == 0 else firsts[i][b]
                    term = conj_product(signal[i - d, b, at], signal_grad[i, b, at])
                    total = term if total is None else total + term
        lines[:, d * 256 : (d + 1) * 256] = total
    sums = lax.dot_general(
        table[...], lines[...], (((1,), (1,)), ((), ())), precision=lax.Precision.HIGHEST, preferred_element_type=F32
    )
    aligned = jnp.sum(sums * tap_values[...], axis=0, keepdims=True)
    skip = jnp.zeros((OWNED, 256), F32)
    for j in range(blocks):
        skip += values[j, :OWNED] * grads[j]
    skip = lax.dot_general(
        jnp.ones((8, 256), F32), skip, (((1,), (1,)), ((), ())), precision=lax.Precision.HIGHEST, preferred_element_type=F32
    )
    row = lax.broadcasted_iota(jnp.int32, (8, OWNED), 0)
    extra = jnp.where(row == 0, skip, jnp.where(row == 1, aligned, 0.0))
    for i in range(NSCALE):
        out[i, :KDIM] = sums[i * KDIM : (i + 1) * KDIM]
        out[i, KDIM:] = extra


def project(h, gain, w_in, normed_out, gate_out, values_out):
    normed = (normalized(h)[0] * gain).astype(BF16)
    normed_out[...] = normed
    weight = w_in[...]
    values = dot(normed, weight[:, :D]).astype(BF16).astype(F32)
    values_out[:, :OWNED] = values.T.reshape(values_out.shape[0], OWNED, TOKENS)
    values_out.send()
    gate_out[...] = dot(normed, weight[:, D:])


def first_kernel(acts, seg, gain, w_in, normed_out, gate_out, values_out):
    ids = jnp.concatenate([seg[0:1], seg[1:2]], axis=1).astype(F32)
    values_out[:, OWNED:] = jnp.broadcast_to(ids[None], (values_out.shape[0], 8, TOKENS))
    project(acts[...].astype(F32), gain[0:1], w_in, normed_out, gate_out, values_out)


def mixer_and_ffn(conv, gate, h, w_out, gain, w_up, w_down, gated_out, middle_out, normed_out, active_out, slope_out, keep):
    conv_out = conv[...].reshape(D, 256).T
    value, slope = gelu_pair(gate[...])
    keep(value, conv_out * slope)
    gated = (conv_out * value).astype(BF16)
    gated_out[...] = gated
    middle = h[...].astype(F32) + dot(gated, w_out[...])
    middle_out[...] = middle
    normed = (normalized(middle)[0] * gain).astype(BF16)
    normed_out[...] = normed
    total = middle
    for n in range(4):
        at = slice(n * 512, (n + 1) * 512)
        value, slope = gelu_pair(dot(normed, w_up[:, at]))
        active = value.astype(BF16)
        active_out[:, at] = active
        slope_out[:, at] = slope.astype(slope_out.dtype)
        total = total + dot(active, w_down[at, :])
    return total


def middle_kernel(conv, gate, h, w_out, gain_two, w_up, w_down, gain_one, w_in, gated_out, middle_out, normed_two_out, active_out,
                  slope_out, gate_value_out, gate_slope_out, state_out, normed_out, gate_out, values_out):
    def keep(value, slope):
        gate_value_out[...] = value
        gate_slope_out[...] = slope
        gate_value_out.send()
        gate_slope_out.send()

    state = mixer_and_ffn(conv, gate, h, w_out, gain_two[0:1], w_up, w_down, gated_out, middle_out, normed_two_out, active_out, slope_out, keep)
    state_out[...] = state
    project(state, gain_one[1:2], w_in, normed_out, gate_out, values_out)


LOW, LIFTED, MID, GATE, GRADS = 0, D, D + FF, 2 * D + FF, 3 * D + FF


def rounded(x):
    return x.astype(BF16).astype(F32)


def ffn_back(grad_state, slope, middle, gain, w_up, w_down, w_out, gate_value, gate_slope, grads_out, gate_grad_out, grad_mid_out, grad_conv_out):
    grad_low = grad_state.astype(BF16)
    grads_out[:, LOW:LIFTED] = grad_low.astype(F32)
    grad_normed = None
    for n in range(4):
        at = slice(n * 512, (n + 1) * 512)
        grad_active = dot_nt(grad_low, w_down[at, :])
        lifted = (grad_active * slope[:, at].astype(F32)).astype(BF16)
        grads_out[:, LIFTED + n * 512 : LIFTED + (n + 1) * 512] = lifted.astype(F32)
        term = dot_nt(lifted, w_up[:, at])
        grad_normed = term if grad_normed is None else grad_normed + term
    grad_middle = grad_state + norm_back(grad_normed, middle[...], gain)
    grad_mid_out[...] = grad_middle
    low = grad_middle.astype(BF16)
    grads_out[:, MID:GATE] = low.astype(F32)
    grad_gated = dot_nt(low, w_out[...])
    gate_grad = (grad_gated * gate_slope[...]).astype(BF16)
    gate_grad_out[...] = gate_grad
    grads_out[:, GATE:] = gate_grad.astype(F32)
    grads_out.send()
    grad_conv_out[...] = (grad_gated * gate_value[...]).T.reshape(grad_conv_out.shape)


def top_kernel(conv, gate, h, w_out, gain_two, w_up, w_down, cotangent, act_out, gated_out, normed_two_out, active_out,
               grads_out, gate_grad_out, grad_mid_out, grad_conv_out, middle, slope, gate_value, gate_slope):
    gain_two = gain_two[1:2]

    def keep(value, slope_part):
        gate_value[...] = value
        gate_slope[...] = slope_part

    act_out[...] = mixer_and_ffn(conv, gate, h, w_out, gain_two, w_up, w_down, gated_out, middle, normed_two_out, active_out, slope, keep)
    ffn_back(cotangent[...].astype(F32), slope, middle, gain_two, w_up, w_down, w_out, gate_value, gate_slope,
             grads_out, gate_grad_out, grad_mid_out, grad_conv_out)


def mixer_back(grad_values, gate_grad, grad_middle, h, gain, w_in, values_out):
    values = grad_values[...].reshape(D, TOKENS).T.astype(BF16)
    values_out[...] = values.astype(F32)
    values_out.send()
    grad_normed = dot_nt(values, w_in[:, :D]) + dot_nt(gate_grad[...], w_in[:, D:])
    return grad_middle[...] + norm_back(grad_normed, h[...].astype(F32), gain)


def between_kernel(grad_values, gate_grad, grad_middle, h, gain_one, w_in, slope, middle, gain_two, w_up, w_down, w_out, gate_value,
                   gate_slope, values_out, grads_out, gate_grad_out, grad_mid_out, grad_conv_out):
    state = mixer_back(grad_values, gate_grad, grad_middle, h, gain_one[1:2], w_in, values_out)
    ffn_back(state, slope, middle, gain_two[0:1], w_up, w_down, w_out, gate_value, gate_slope, grads_out, gate_grad_out, grad_mid_out,
             grad_conv_out)


def last_kernel(grad_values, gate_grad, grad_middle, h, gain_one, w_in, values_out, grad_out):
    grad_out[...] = mixer_back(grad_values, gate_grad, grad_middle, h, gain_one[0:1], w_in, values_out)


def split_kernel(normed_one, gated, normed_two, active, own_out, send_out):
    first = lax.axis_index("rows") % 2 == 0
    at = 0
    for x, step in ((normed_one, 64), (gated, 64), (normed_two, 64), (active, 256)):
        lines = x[...].astype(F32).T
        for z in range(4):
            even = lines[2 * z * step : (2 * z + 1) * step]
            odd = lines[(2 * z + 1) * step : (2 * z + 2) * step]
            own_out[at : at + step, :] = jnp.where(first, even, odd).astype(BF16)
            send_out[at : at + step, :] = jnp.where(first, odd, even)
            at += step


def store_wide(out, at, left, right):
    width = left.shape[1]
    left = left.reshape(32, 8, width)
    right = right.reshape(32, 8, width)
    low = lax.broadcasted_iota(jnp.int32, (32, 8, width), 1) < 4
    even = jnp.where(low, left, pltpu.roll(right, 4, 1))
    odd = jnp.where(low, pltpu.roll(left, 4, 1), right)
    both = jnp.stack([even, odd], axis=1).reshape(4, 16, 8, width)
    for n in range(width // 128):
        out[:, :, at + n * 8 : at + (n + 1) * 8, :] = both[:, :, :, n * 128 : (n + 1) * 128]


def pair_product(own, other, rows, grads, other_grads, columns):
    return dot(own[rows, :], grads[:, columns].astype(BF16)) + dot(other[rows, :].astype(BF16), other_grads[:, columns].astype(BF16))


def wide_product(out, at, own, other, rows, grads, other_grads, left, right, width):
    left = pair_product(own, other, rows, grads, other_grads, slice(left, left + width))
    right = pair_product(own, other, rows, grads, other_grads, slice(right, right + width))
    store_wide(out, at, left, right)


ROWS_IN, ROWS_OUT, ROWS_UP, ROWS_DOWN = slice(0, 256), slice(256, 512), slice(512, 768), 768
AT_DOWN, AT_UP, AT_OUT, AT_GATE, AT_VALUES, LINES = 0, 64, 128, 144, 160, 176


def weight_lines(own, other, grads, other_grads, lines, done):
    for n in range(4):
        rows = slice(ROWS_DOWN + n * 256, ROWS_DOWN + (n + 1) * 256)
        down = pair_product(own, other, rows, grads, other_grads, slice(LOW, LIFTED)).reshape(16, 16, D)
        for half in range(2):
            for lane in range(4):
                at = AT_DOWN + half * 32 + lane * 8
                lines[n, :, at : at + 8, :] = down[:, half * 8 : half * 8 + 8, lane * 128 : (lane + 1) * 128]
    done(AT_DOWN, AT_UP)
    for n in range(4):
        wide_product(lines, AT_UP + n * 16, own, other, ROWS_UP, grads, other_grads, LIFTED + n * 256, LIFTED + 1024 + n * 256, 256)
    done(AT_UP, AT_OUT)
    wide_product(lines, AT_OUT, own, other, ROWS_OUT, grads, other_grads, MID, MID + 256, 256)
    wide_product(lines, AT_GATE, own, other, ROWS_IN, grads, other_grads, GATE, GATE + 256, 256)


def ring_parts(lines, here, to_right, to_left, right, left):
    z = lax.axis_index("rows") // 2
    at = lambda step: lines.at[lax.rem(z + step, 4)]
    first, second = pl.ds(0, 8), pl.ds(8, 8)
    return [
        (at(2).at[first], to_right.at[first]),
        (at(1).at[second], to_right.at[second]),
        (at(3).at[first], to_left.at[first]),
        (at(2).at[second], to_left.at[second]),
        (at(1).at[first], right),
        (at(3).at[second], left),
        (at(0), here),
    ]


class Sending:
    def __init__(self, pairs, sems):
        self.pairs, self.sems, self.copies = pairs, sems, []

    def __call__(self, start, end):
        lines = pl.ds(start, end - start)
        for source, target in self.pairs:
            copy = pltpu.make_async_copy(source.at[:, lines], target.at[:, lines], self.sems.at[len(self.copies)])
            copy.start()
            self.copies.append(copy)

    def wait(self):
        for copy in self.copies:
            copy.wait()


def weight_kernel(own, other, grads, other_grads, out, lines, sems):
    send = Sending([(lines.at[z], out.at[:, z]) for z in range(4)], sems)
    weight_lines(own, other, grads, other_grads, lines, send)
    send(AT_OUT, AT_VALUES)
    send.wait()


def weight_ring_kernel(own, other, grads, other_grads, late_own, late_other, late_grads, late_other_grads, *rest):
    *outs, lines, sems = rest
    send = Sending(ring_parts(lines, *outs), sems)
    wide_product(lines, AT_VALUES, late_own, late_other, ROWS_IN, late_grads, late_other_grads, 0, 256, 256)
    weight_lines(own, other, grads, other_grads, lines, send)
    send(AT_OUT, LINES)
    send.wait()


def last_weight_kernel(own, other, grads, other_grads, *rest):
    *outs, lines, sems = rest
    z = lax.axis_index("rows") // 2
    send = Sending([(lines.at[lax.rem(z + step, 4)], out) for step, out in enumerate(outs)], sems)
    wide_product(lines, 0, own, other, ROWS_IN, grads, other_grads, 0, 256, 256)
    send(0, 16)
    send.wait()


def unpack_kernel(*refs):
    parts_one, (parts_zero, w_in, w_up, in_out, up_out, out_out, down_out, gain_one_out, gain_two_out) = refs[:4], refs[4:]
    lines_one = parts_one[0][...] + parts_one[1][...] + parts_one[2][...] + parts_one[3][...]
    lines_zero = parts_zero[0]
    for j in range(1, parts_zero.shape[0]):
        lines_zero = lines_zero + parts_zero[j]

    def wide(target, l, lines, at, column, gap):
        for n in range(2):
            for half in range(2):
                to = column + half * gap + n * 128
                target[l, :, to : to + 128] = lines[at + n * 8 + half * 4 : at + n * 8 + half * 4 + 4, :]

    for l, lines in ((0, lines_zero), (1, lines_one)):
        for half in range(2):
            for lane in range(4):
                at = AT_DOWN + half * 32 + lane * 8
                down_out[l, half * 8 : half * 8 + 8, lane * 128 : (lane + 1) * 128] = lines[at : at + 8, :]
        for n in range(4):
            wide(up_out, l, lines, AT_UP + n * 16, n * 256, 1024)
        wide(out_out, l, lines, AT_OUT, 0, 256)
        wide(in_out, l, lines, AT_GATE, D, 256)
    wide(in_out, 0, lines_zero, LINES, 0, 256)
    wide(in_out, 1, lines_zero, AT_VALUES, 0, 256)
    for l in range(LAYERS):
        one = jnp.sum(in_out[l] * w_in[l].astype(F32), axis=1, keepdims=True)
        two = jnp.sum(up_out[l] * w_up[l].astype(F32), axis=1, keepdims=True)
        gain_one_out[l] = jnp.broadcast_to(one, (4, 128))
        gain_two_out[l] = jnp.broadcast_to(two, (4, 128))


def place(axis):
    rows, seq = lax.axis_index("rows"), lax.axis_index("seq")
    return {"z": rows // 2, "core": rows % 2, "y": seq // 4, "x": seq % 4}[axis]


def shift(x, axis, step):
    if axis == "core":
        return lax.ppermute(x, "rows", [(i, i ^ 1) for i in range(8)])
    if axis == "z":
        return lax.ppermute(x, "rows", [(i, (i + 2 * step) % 8) for i in range(8)])
    if axis == "y":
        return lax.ppermute(x, "seq", [(i, (i + 4 * step) % 16) for i in range(16)])
    return lax.ppermute(x, "seq", [(i, i // 4 * 4 + (i + step) % 4) for i in range(16)])


def direct_parts(x, axis):
    take = lambda step: lax.dynamic_index_in_dim(x, (place(axis) + step) % 4, 0, False)
    return [take(0)] + [shift(take(step), axis, step) for step in (1, 3, 2)]


def exchange_all(x, axis):
    return lax.all_to_all(x, axis, 0, 0, tiled=True)


def to_everyone(x, axis):
    return exchange_all(jnp.broadcast_to(x[None], (lax.axis_size(axis), *x.shape)), axis)


def per_device(acts, segment_ids, cotangent, norm_one, w_in, taps, skip_gain, w_out, norm_two, w_up, w_down):
    seq = lax.axis_index("seq")
    rows = lax.axis_index("rows")
    blocks = lax.axis_size("seq")
    owner = (rows * blocks + seq) * 4
    into_np, back_np, table_np = build_tables(blocks)
    into = jnp.asarray(into_np, BF16)
    back = jnp.asarray(back_np, BF16)
    into_grad = jnp.asarray(back_np.T, BF16)
    back_grad = jnp.asarray(into_np.T, BF16)
    table = jnp.asarray(table_np, F32)

    state = acts.reshape(TOKENS, D)
    exchange = (blocks, OWNED, TOKENS)
    wide = lambda n, t: ((TOKENS, n), t)
    room = lambda *shapes: [pltpu.VMEM(s, t) for s, t in shapes]

    def swap(x):
        return lax.all_to_all(x, "seq", 0, 0, tiled=True)

    normed_one, gate, values = call(
        first_kernel,
        [wide(D, BF16), wide(D, F32), ((blocks, OWNED + 8, TOKENS), F32)],
        (state, segment_ids, norm_one, (w_in, 0)),
        flops=2 * 10**9,
    )
    values_zero = seg = swap(values)

    taps_here = lax.dynamic_slice_in_dim(taps[:, 0], seq * OWNED, OWNED, 2)
    taps_all = to_everyone(taps_here.reshape(LAYERS * KDIM, OWNED), "rows")
    shapes = [((128, OWNED), F32), ((1, OWNED), F32), ((blocks, OWNED, 256), F32)]
    tap_parts = call(
        spectra_kernel,
        [s for s in shapes for _ in range(LAYERS)],
        (taps_all, jnp.asarray(TAP_DECAY), jnp.asarray(TAP_REPEAT), table),
        flops=10**9,
    )
    tap_values, norms, spectra = tap_parts[:LAYERS], tap_parts[LAYERS : 2 * LAYERS], tap_parts[2 * LAYERS :]
    skip_here = lax.dynamic_slice_in_dim(skip_gain, seq * OWNED, OWNED, 1)
    skip_here = jnp.broadcast_to(skip_here[:, :, None], (LAYERS, OWNED, 128))

    def conv(l, forward, source, after):
        first, second = (into, back) if forward else (into_grad, back_grad)
        (out,) = call(
            lambda *refs: conv_kernel(forward, *refs),
            [(exchange, F32)],
            (seg, source, first, spectra[l], (skip_here, l), second, (after, None)),
            scratch=room(((blocks, 2, DOCS, OWNED, 256), F32), ((2, 2, DOCS, OWNED, 256), F32)),
            flops=4 * 10**9,
        )
        return out

    def split(*args):
        own, send = call(split_kernel, [((1792, TOKENS), BF16), ((1792, TOKENS), F32)], args, flops=2 * 10**9)
        return own, shift(send, "core", 1)

    conv_zero = swap(conv(0, True, values_zero, seg))
    (gated_zero, middle_zero, normed_two_zero, active_zero, slope_zero, gate_value_zero, gate_slope_zero, state_one, normed_one_one,
     gate_one, values_one) = call(
        middle_kernel,
        [wide(D, BF16), wide(D, F32), wide(D, BF16), wide(FF, BF16), wide(FF, BF16), wide(D, F32), wide(D, F32), wide(D, F32),
         wide(D, BF16), wide(D, F32), (exchange, F32)],
        (conv_zero, gate, state, (w_out, 0), norm_two, (w_up, 0), (w_down, 0), norm_one, (w_in, 1)),
        flops=4 * 10**9,
    )
    values_one = swap(values_one)
    left_zero = split(normed_one, gated_zero, normed_two_zero, active_zero)
    conv_one = swap(conv(1, True, values_one, left_zero[0]))
    back_outs = [wide(GRADS, F32), wide(D, BF16), wide(D, F32), (exchange, F32)]
    act_out, gated_one, normed_two_one, active_one, grads_one, gate_grad, grad_mid, grad_conv = call(
        top_kernel,
        [wide(D, F32), wide(D, BF16), wide(D, BF16), wide(FF, BF16)] + back_outs,
        (conv_one, gate_one, state_one, (w_out, 1), norm_two, (w_up, 1), (w_down, 1), cotangent.reshape(TOKENS, D)),
        scratch=room(wide(D, F32), wide(FF, BF16), wide(D, F32), wide(D, F32)),
        flops=5 * 10**9,
    )

    def pair_grads(grads):
        return grads, shift(grads, "core", 1)

    def conv_weights(l, source, grads):
        (out,) = call(
            conv_weight_kernel,
            [((NSCALE, KDIM + 8, OWNED), F32)],
            (seg, source, grads, into, into_grad, table, tap_values[l]),
            scratch=room(*[((blocks, 2, DOCS, OWNED, 256), F32)] * 2, ((OWNED, blocks * 256), F32)),
            flops=4 * 10**9,
        )
        return out

    grad_conv = swap(grad_conv)
    left_one = split(normed_one_one, gated_one, normed_two_one, active_one)
    (lines_one,) = call(
        weight_kernel,
        [((blocks, 4, AT_VALUES, 128), F32)],
        (*left_one, *pair_grads(grads_one)),
        scratch=room(((4, blocks, AT_VALUES, 128), F32)) + [pltpu.SemaphoreType.DMA((12,))],
        flops=5 * 10**9,
        raw=True,
    )
    grad_values = swap(conv(1, False, grad_conv, lines_one))
    lines_one = lax.psum_scatter(lines_one.reshape(-1, 128), "seq", tiled=True).reshape(4, AT_VALUES, 128)
    tap_one = conv_weights(1, values_one, grad_conv)
    values_grad_one, grads_zero, gate_grad, grad_mid, grad_conv = call(
        between_kernel,
        [wide(D, F32)] + back_outs,
        (grad_values, gate_grad, grad_mid, state_one, norm_one, (w_in, 1), slope_zero, middle_zero, norm_two, (w_up, 0), (w_down, 0),
         (w_out, 0), gate_value_zero, gate_slope_zero, (tap_one, None)),
        flops=4 * 10**9,
    )
    grad_conv = swap(grad_conv)
    full, half = ((blocks, LINES, 128), F32), ((blocks // 2, LINES, 128), F32)
    here, to_right, to_left, right, left = call(
        weight_ring_kernel,
        [full, full, full, half, half],
        (*left_zero, *pair_grads(grads_zero), *[(x, slice(0, 256)) for x in left_one], *pair_grads(values_grad_one)),
        scratch=room(((4, blocks, LINES, 128), F32)) + [pltpu.SemaphoreType.DMA((21,))],
        flops=6 * 10**9,
        raw=True,
    )
    from_left, from_right = shift(to_right, "z", 1), shift(to_left, "z", 3)
    grad_values = swap(conv(0, False, grad_conv, here))
    tap_zero = conv_weights(0, values_zero, grad_conv)
    values_grad_zero, grad_input = call(
        last_kernel,
        [wide(D, F32), wide(D, F32)],
        (grad_values, gate_grad, grad_mid, state, norm_one, (w_in, 0)),
        flops=3 * 10**9,
    )
    part = ((blocks, 16, 128), F32)
    tail = call(
        last_weight_kernel,
        [part] * 4,
        (*[(x, slice(0, 256)) for x in left_zero], *pair_grads(values_grad_zero)),
        scratch=room(((4, blocks, 16, 128), F32)) + [pltpu.SemaphoreType.DMA((4,))],
        flops=10**9,
        raw=True,
    )
    tail = tail[0] + shift(tail[1], "z", 1) + shift(tail[3], "z", 3) + shift(tail[2], "z", 2)
    middle = blocks // 2
    on_left = shift(right + from_left[:middle], "z", 1)
    on_right = shift(left + from_right[middle:], "z", 3)
    lines_zero = jnp.concatenate(
        [here[:middle] + from_right[:middle] + on_left, here[middle:] + from_left[middle:] + on_right], axis=0
    )
    lines_zero = exchange_all(jnp.concatenate([lines_zero, tail], axis=1), "seq")

    sums = jnp.stack([tap_zero, tap_one], axis=1)
    sums = jnp.sum(exchange_all(sums, "rows"), axis=0)
    decay = lax.dynamic_index_in_dim(jnp.asarray(TAP_DECAY[::KDIM, 0]), rows, 0, False)
    repeat = lax.dynamic_index_in_dim(jnp.asarray(TAP_REPEAT[::KDIM, 0]), rows, 0, False)
    norms = jnp.stack(norms)
    own_values = taps_here * decay * norms
    tap_grad = decay * norms * (sums[:, :KDIM] - repeat * own_values * sums[:, KDIM + 1 : KDIM + 2])
    small = jnp.concatenate([tap_grad, sums[:, KDIM:]], axis=1)
    small = to_everyone(small, "seq").transpose(1, 2, 0, 3).reshape(LAYERS, KDIM + 8, D)

    mine = lambda x, dim: lax.dynamic_slice_in_dim(x, owner, 4, dim)
    in_grad, up_grad, out_grad, down_grad, gain_one, gain_two = call(
        unpack_kernel,
        [((LAYERS, 4, 2 * D), F32), ((LAYERS, 4, FF), F32), ((LAYERS, 4, D), F32), ((LAYERS, 16, D), F32), ((LAYERS, 4, 128), F32),
         ((LAYERS, 4, 128), F32)],
        (*direct_parts(lines_one, "z"), lines_zero, mine(w_in, 1), mine(w_up, 1)),
    )
    return (
        act_out.reshape(acts.shape),
        grad_input.reshape(acts.shape),
        gain_one[:, :, 0] / mine(norm_one, 1),
        in_grad,
        small[:, None, :KDIM, :],
        mine(small[:, KDIM], 1),
        out_grad,
        gain_two[:, :, 0] / mine(norm_two, 1),
        up_grad,
        down_grad,
    )


def solution(mesh):
    wide = P("rows", "seq", None)
    in_specs = (wide, P("rows", "seq"), wide, P(), P(), P(None, "rows", None, None), P(), P(), P(), P(), P())
    split = P(None, ("rows", "seq"))
    split_wide = P(None, ("rows", "seq"), None)
    out_specs = (wide, wide, split, split_wide, P(None, "rows", None, None), split, split_wide, split, split_wide, split_wide)
    return jax.shard_map(per_device, mesh=mesh, in_specs=in_specs, out_specs=out_specs, check_vma=False)
```
